32 devices in a mesh: blk: 8 (over z, core), split: 4 (over y, x).
Axes of the slice: x: 2, y: 2, z: 4, core: 2. Of those that a mesh axis runs over, the one named last changes fastest.
Arguments:
- orbitals: float32 [4096, 512], P('blk'), may hold values from -6 to 6
- kernel: float32 [4096, 4, 1024], P('blk', 'split'), as said below
Outputs:
- exchange_out: float32 [4096, 512], P(('blk', 'split'))
The draws below stay inside these ranges and needn't reach their ends.
Inputs may be any that keep to these rules, and one draw needn't show every extreme that they name: Z built from kernel as in the first step is a symmetric matrix.
All inputs are finite; a program needn't handle non-finite values.
Results may differ from the reference program's by a relative error of at most 0.00013.
Values sent between devices are 32-bit elements; how exact they have to be, the bound alone decides.
No kernel may reach another device: no remote copies, remote signals or barrier semaphores. Data moves between devices by JAX's collectives and lax.ppermute only.
A program may use at most 64 MiB of HBM per device.

```python
import jax
import jax.numpy as jnp
from jax import lax

NORB = 512
PB = 512
NPTS = 4096
SHARE = 128
N_BLK = 8
N_SPLIT = 4


def draw_kernel(key, part):
    total = NPTS
    first = jax.random.normal(jax.random.fold_in(key, 11), (total, total), jnp.float32)
    sym = (first + first.T) * 0.5 ** 0.5
    sym = sym / jnp.sqrt(jnp.float32(total * NORB))
    sym = sym.reshape(total, N_BLK, N_SPLIT, SHARE)
    sym = jnp.transpose(sym, (0, 2, 1, 3))
    return sym.reshape(total, N_SPLIT, N_BLK * SHARE)


def level_of(stream_key, shape, cuts, low, top_value):
    level, own = 1.0, jax.random.fold_in(stream_key, 6)
    for axis_at, shards_of in cuts:
        heights = jnp.exp(jax.random.uniform(jax.random.fold_in(own, axis_at), (shards_of,), jnp.float32, low / len(cuts), top_value / len(cuts)))
        level = level * jnp.repeat(heights, shape[axis_at] // shards_of).reshape([-1 if axis == axis_at else 1 for axis in range(len(shape))])
    return level


def normal_values(own_key, shape, spread, limit, split=(), kind=jnp.bfloat16):
    gain = level_of(own_key, shape, split, -0.22, 0.18) if split else 1.0
    array = jax.random.normal(own_key, shape, jnp.float32) * spread * gain
    return jnp.minimum(jnp.maximum(array, -limit), limit).astype(kind)


def setup_inputs(seed: int = 0) -> dict:
    keys = jax.random.split(jax.random.key(seed), 3)
    return {
        "orbitals": normal_values(keys[0], (NPTS, NORB), 1.0, 6.0, ((0, 8),), jnp.float32),
        "kernel": draw_kernel(jax.random.fold_in(keys[2], 71), 0),
    }


def reference(orbitals, kernel):
    blocks_orb = orbitals.reshape(N_BLK, PB, NORB)
    blocks_ker = kernel.reshape(N_BLK, PB, N_SPLIT, N_BLK, SHARE)

    def one_block(pieces):
        rows_orb, rows_ker = pieces
        z_rows = jnp.transpose(rows_ker, (0, 2, 1, 3)).reshape(PB, NPTS)
        density = jnp.dot(rows_orb, orbitals.T, precision=lax.Precision.HIGHEST, preferred_element_type=jnp.float32)
        weighted = z_rows * density
        return jnp.dot(weighted, orbitals, precision=lax.Precision.HIGHEST, preferred_element_type=jnp.float32)

    result = lax.map(one_block, (blocks_orb, blocks_ker))
    return result.reshape(NPTS, NORB)
```

```python
import jax
import jax.numpy as jnp
from jax import lax
from jax.sharding import PartitionSpec as P

CORES = 2


def product(a, b, dims):
    return lax.dot_general(
        a, b, (dims, ((), ())), precision=lax.Precision.HIGH, preferred_element_type=jnp.float32
    )


def per_device(orbitals, kernel):
    nchips = lax.axis_size("blk") // CORES
    nshares = lax.axis_size("split")
    q = lax.axis_index("blk")
    share_id = lax.axis_index("split")
    chip, core = q // CORES, q % CORES
    share = orbitals.shape[0] // nshares
    width = CORES * share
    half = nchips // 2
    z_rows = kernel[:, 0, :]

    def is_inner(c):
        return abs(2 * c - nchips + 1) < half

    inner_chips = [c for c in range(nchips) if is_inner(c)]
    outer_chips = [c for c in range(nchips) if not is_inner(c)]
    inner = jnp.abs(2 * chip - nchips + 1) < half

    def along(value, pairs):
        full = [(CORES * a + c, CORES * b + c) for a, b in pairs for c in range(CORES)]
        return lax.ppermute(value, "blk", full)

    def other_core(value):
        return lax.ppermute(value, "blk", [(i, i ^ 1) for i in range(nchips * CORES)])

    def in_order(mine, other):
        first = jnp.where(core == 0, mine, other)
        second = jnp.where(core == 0, other, mine)
        return jnp.concatenate([first, second], axis=0)

    own = lax.dynamic_slice_in_dim(orbitals, share_id * share, share, 0)
    far = along(own, [(c, c ^ half) for c in outer_chips])
    arrived = {}
    for k in range(1, half):
        arrived[k] = along(own, [(c, c ^ k) for c in range(nchips)])
    for k in range(half + 1, nchips):
        arrived[k] = along(own, [(c, c ^ k) for c in inner_chips])

    def weighted(k, points):
        z_part = lax.dynamic_slice_in_dim(z_rows, (chip ^ k) * width, width, 1)
        return z_part * product(orbitals, points, ((1,), (1,)))

    def rows_of(weights, points):
        return product(weights, points, ((1,), (0,)))

    points = in_order(own, other_core(own))
    total = rows_of(weighted(0, points), points)

    points = in_order(far, other_core(far))
    weights = weighted(half, points)
    back = product(weights, orbitals, ((0,), (0,)))
    mine = lax.dynamic_slice_in_dim(back, core * share, share, 0)
    theirs = lax.dynamic_slice_in_dim(back, (1 - core) * share, share, 0)
    returned = along(mine + other_core(theirs), [(c, c ^ half) for c in inner_chips])
    total += rows_of(weights, points)

    for k in range(1, half):
        points = in_order(arrived[k], other_core(arrived[k]))
        total += rows_of(weighted(k, points), points)
    for k in range(half + 1, nchips):
        passed = along(far, [(c, c ^ half ^ k) for c in inner_chips])
        here = jnp.where(inner, arrived[k], passed)
        points = in_order(here, other_core(here))
        total += rows_of(weighted(k, points), points)

    bits = nshares.bit_length() - 1
    ncols = orbitals.shape[1] // bits
    parts = []
    for part in range(bits):
        held = total[:, part * ncols : (part + 1) * ncols].reshape((2,) * bits + (share, ncols))
        for step in range(bits):
            bit = (part + step) % bits
            axis = bits - 1 - bit
            my_bit = (share_id >> bit) & 1
            keep = lax.dynamic_slice_in_dim(held, my_bit, 1, axis)
            send = lax.dynamic_slice_in_dim(held, 1 - my_bit, 1, axis)
            got = lax.ppermute(send, "split", [(i, i ^ (1 << bit)) for i in range(nshares)])
            held = keep + got
        parts.append(held.reshape(share, ncols))
    return jnp.concatenate(parts, axis=1) + returned


def solution(mesh):
    placed = (P("blk", None), P("blk", "split", None))
    return jax.shard_map(
        per_device, mesh=mesh, in_specs=placed, out_specs=P(("blk", "split"), None), check_vma=False
    )
```

```python
import jax
import jax.numpy as jnp
from jax import lax
from jax.experimental import pallas as pl
from jax.experimental.pallas import tpu as pltpu
from jax.sharding import PartitionSpec as P

CORES = 2
LANES = 128
MIB = 1 << 20


def product(a, b, dims):
    return lax.dot_general(
        a, b, (dims, ((), ())), precision=lax.Precision.HIGH, preferred_element_type=jnp.float32
    )


def pick_body(at_ref, kernel_ref, *out_refs):
    share = out_refs[0].shape[1] // CORES
    for i, out_ref in enumerate(out_refs):
        for c in range(CORES):
            start = pl.multiple_of(at_ref[i * CORES + c] * share, share)
            out_ref[:, c * share : (c + 1) * share] = kernel_ref[:, 0, pl.ds(start, share)]


def pick_columns(kernel, blocks, share):
    rows, count = kernel.shape[0], len(blocks) // CORES
    if share % LANES:
        flat = kernel[:, 0, :]
        parts = [lax.dynamic_slice_in_dim(flat, b * share, share, 1) for b in blocks]
        return [jnp.concatenate(parts[i * CORES : (i + 1) * CORES], axis=1) for i in range(count)]
    return pl.pallas_call(
        pick_body,
        in_specs=[
            pl.BlockSpec(memory_space=pltpu.SMEM),
            pl.BlockSpec(memory_space=pltpu.VMEM),
        ],
        out_specs=[pl.BlockSpec(memory_space=pltpu.VMEM)] * count,
        out_shape=[jax.ShapeDtypeStruct((rows, CORES * share), jnp.float32)] * count,
        compiler_params=pltpu.CompilerParams(vmem_limit_bytes=16 * MIB),
        cost_estimate=pl.CostEstimate(flops=0, bytes_accessed=4 * kernel.size, transcendentals=0),
    )(jnp.stack(blocks).astype(jnp.int32), kernel)


def per_device(orbitals, kernel):
    nchips = lax.axis_size("blk") // CORES
    nshares = lax.axis_size("split")
    q = lax.axis_index("blk")
    share_id = lax.axis_index("split")
    chip = q // CORES
    share = orbitals.shape[0] // nshares
    half, near = nchips // 2, nchips // 4
    across = half ^ near

    def is_inner(c):
        return (c // half) != (c // near) % 2

    inner_chips = [c for c in range(nchips) if is_inner(c)]
    outer_chips = [c for c in range(nchips) if not is_inner(c)]
    inner = (chip // half) != (chip // near) % 2

    def along(value, pairs):
        full = [(CORES * a + c, CORES * b + c) for a, b in pairs for c in range(CORES)]
        return lax.ppermute(value, "blk", full)

    def other_core(value):
        return lax.ppermute(value, "blk", [(i, i ^ 1) for i in range(nchips * CORES)])

    own = lax.dynamic_slice_in_dim(orbitals, share_id * share, share, 0)
    pair_own = other_core(own)
    x = along(own, [(c, c ^ half) for c in outer_chips] + [(c, c ^ near) for c in inner_chips])

    others = [k for k in range(1, nchips) if k not in (near, half, across)]
    blocks = []
    for k in [0, jnp.where(inner, half, near), across] + others:
        blocks += [q ^ (CORES * k), q ^ (CORES * k + 1)]
    z_own, z_x, z_late, *z_others = pick_columns(kernel, blocks, share)

    def weighted(z_part, points):
        return z_part * product(orbitals, points, ((1,), (1,)))

    def rows_of(weights, points):
        return product(weights, points, ((1,), (0,)))

    points = jnp.concatenate([own, pair_own], axis=0)
    total = rows_of(weighted(z_own, points), points)

    own_late, z_x, z_late = lax.optimization_barrier((own, z_x, z_late))
    swapped = along(own_late, [(c, c ^ across) for c in inner_chips])

    for k, z_k in zip(others, z_others):
        more = along(own_late, [(c, c ^ k) for c in range(nchips)])
        points = jnp.concatenate([more, other_core(more)], axis=0)
        total += rows_of(weighted(z_k, points), points)

    passed = along(x, [(c, c ^ near) for c in range(nchips)])
    points = jnp.concatenate([x, other_core(x)], axis=0)
    weights = weighted(z_x, points)
    back = product(weights, orbitals, ((0,), (0,)))
    back = back[:share] + other_core(back[share:])
    total += rows_of(weights, points)

    total, back, passed, swapped = lax.optimization_barrier((total, back, passed, swapped))
    late = jnp.where(inner, swapped, passed)
    late, back = lax.optimization_barrier((late, back))
    points = jnp.concatenate([late, other_core(late)], axis=0)
    returned = along(
        back, [(c, c ^ half) for c in inner_chips] + [(c, c ^ near) for c in outer_chips]
    )
    total += rows_of(weighted(z_late, points), points)

    def for_share(at):
        return lax.dynamic_slice_in_dim(total, at * share, share, 0)

    out = for_share(share_id) + returned
    masks = sorted(range(1, nshares), key=lambda mask: -mask.bit_count())
    for mask in masks:
        out += lax.ppermute(
            for_share(share_id ^ mask), "split", [(i, i ^ mask) for i in range(nshares)]
        )
    return out


def solution(mesh):
    placed = (P("blk", None), P("blk", "split", None))
    return jax.shard_map(
        per_device, mesh=mesh, in_specs=placed, out_specs=P(("blk", "split"), None), check_vma=False
    )
```

```python
import jax
import jax.numpy as jnp
from jax import lax
from jax.experimental import pallas as pl
from jax.experimental.pallas import tpu as pltpu
from jax.sharding import PartitionSpec as P

CORES = 2
CHUNKS = 2
LANES = 128
MIB = 1 << 20


def product(a, b, dims):
    return lax.dot_general(
        a, b, (dims, ((), ())), precision=lax.Precision.HIGH, preferred_element_type=jnp.float32
    )


def pick_body(at_ref, kernel_ref, *out_refs):
    share = out_refs[0].shape[1] // CORES
    for i, out_ref in enumerate(out_refs):
        for c in range(CORES):
            start = pl.multiple_of(at_ref[i * CORES + c] * share, share)
            out_ref[:, c * share : (c + 1) * share] = kernel_ref[:, 0, pl.ds(start, share)]


def pick_columns(kernel, blocks, share):
    rows, count = kernel.shape[0], len(blocks) // CORES
    if share % LANES:
        flat = kernel[:, 0, :]
        parts = [lax.dynamic_slice_in_dim(flat, b * share, share, 1) for b in blocks]
        return [jnp.concatenate(parts[i * CORES : (i + 1) * CORES], axis=1) for i in range(count)]
    return pl.pallas_call(
        pick_body,
        in_specs=[
            pl.BlockSpec(memory_space=pltpu.SMEM),
            pl.BlockSpec(memory_space=pltpu.VMEM),
        ],
        out_specs=[pl.BlockSpec(memory_space=pltpu.VMEM)] * count,
        out_shape=[jax.ShapeDtypeStruct((rows, CORES * share), jnp.float32)] * count,
        compiler_params=pltpu.CompilerParams(vmem_limit_bytes=16 * MIB),
        cost_estimate=pl.CostEstimate(flops=0, bytes_accessed=4 * kernel.size, transcendentals=0),
    )(jnp.stack(blocks).astype(jnp.int32), kernel)


def per_device(orbitals, kernel):
    nchips = lax.axis_size("blk") // CORES
    nshares = lax.axis_size("split")
    q = lax.axis_index("blk")
    share_id = lax.axis_index("split")
    chip, core = q // CORES, q % CORES
    share = orbitals.shape[0] // nshares
    steps = nchips // 2

    ring = list(range(0, nchips, 2)) + list(range(1, nchips, 2))[::-1]

    def shift(value, by):
        pairs = [
            (CORES * c + i, CORES * ring[(at + by) % nchips] + i)
            for at, c in enumerate(ring)
            for i in range(CORES)
        ]
        return lax.ppermute(value, "blk", pairs)

    def chip_behind(t):
        at = jnp.where(chip % 2 == 0, chip // 2, nchips - 1 - chip // 2)
        at = (at - t + nchips) % nchips
        return jnp.where(2 * at < nchips, 2 * at, 2 * (nchips - 1 - at) + 1)

    def other_core(value):
        return lax.ppermute(value, "blk", [(i, i ^ 1) for i in range(nchips * CORES)])

    def weighted(z_part, points):
        return z_part * product(orbitals, points, ((1,), (1,)))

    def rows_of(weights, points):
        return product(weights, points, ((1,), (0,)))

    own = lax.dynamic_slice_in_dim(orbitals, share_id * share, share, 0)
    pair_own = other_core(own)
    held = shift(own, 1)

    blocks = []
    for t in range(steps + 1):
        there = CORES * chip_behind(t)
        blocks += [there + core, there + 1 - core]
    z_parts = pick_columns(kernel, blocks, share)

    points = jnp.concatenate([own, pair_own], axis=0)
    total = rows_of(weighted(z_parts[0], points), points)

    backs = []
    for t in range(1, steps):
        points = jnp.concatenate([held, other_core(held)], axis=0)
        ahead = shift(held, 1)
        weights = weighted(z_parts[t], points)
        back = product(weights, orbitals, ((0,), (0,)))
        backs.append(back[:share] + other_core(back[share:]))
        total += rows_of(weights, points)
        held = ahead
    total, backs, held = lax.optimization_barrier((total, backs, held))

    pair_held = other_core(held)
    z_last = z_parts[steps]
    total += rows_of(weighted(z_last[:, :share], held), held)
    total, pair_held = lax.optimization_barrier((total, pair_held))
    total += rows_of(weighted(z_last[:, share:], pair_held), pair_held)
    total, backs = lax.optimization_barrier((total, backs))
    returned = sum(shift(back, -t) for t, back in enumerate(backs, 1))

    bits = nshares.bit_length() - 1

    def bit_at(step, on_core):
        return (step + on_core * (bits // 2)) % bits

    def share_mask(place, on_core):
        return sum(((place >> (bits - 1 - t)) & 1) << bit_at(t, on_core) for t in range(bits))

    masks = [jnp.where(core == 0, share_mask(p, 0), share_mask(p, 1)) for p in range(nshares)]
    cut = orbitals.shape[1] // CHUNKS

    def blocks_of(places, chunk):
        found = [
            lax.dynamic_slice(total, ((share_id ^ masks[p]) * share, chunk * cut), (share, cut))
            for p in places
        ]
        return jnp.concatenate(found, axis=0)

    def halve(keep, send, step):
        pairs = [
            (b * nshares + s, b * nshares + (s ^ (1 << bit_at(step, b % CORES))))
            for b in range(nchips * CORES)
            for s in range(nshares)
        ]
        return keep + lax.ppermute(send, ("blk", "split"), pairs)

    places, middle = list(range(nshares)), nshares // 2
    parts = [halve(blocks_of(places[:middle], k), blocks_of(places[middle:], k), 0) for k in range(CHUNKS)]
    for step in range(1, bits):
        size = parts[0].shape[0] // 2
        parts = [halve(part[:size], part[size:], step) for part in parts]
    return jnp.concatenate(parts, axis=1) + returned


def solution(mesh):
    placed = (P("blk", None), P("blk", "split", None))
    return jax.shard_map(
        per_device, mesh=mesh, in_specs=placed, out_specs=P(("blk", "split"), None), check_vma=False
    )
```

```python
import jax
import jax.numpy as jnp
from jax import lax
from jax.experimental import pallas as pl
from jax.experimental.pallas import tpu as pltpu
from jax.sharding import PartitionSpec as P

CORES = 2
CHUNKS = 2
LANES = 128
MIB = 1 << 20


def product(a, b, dims):
    return lax.dot_general(
        a, b, (dims, ((), ())), precision=lax.Precision.HIGH, preferred_element_type=jnp.float32
    )


def pick_body(at_ref, kernel_ref, *out_refs):
    share = out_refs[0].shape[1] // CORES
    for i, out_ref in enumerate(out_refs):
        for c in range(CORES):
            start = pl.multiple_of(at_ref[i * CORES + c] * share, share)
            out_ref[:, c * share : (c + 1) * share] = kernel_ref[:, 0, pl.ds(start, share)]


def pick_columns(kernel, blocks, share):
    rows, count = kernel.shape[0], len(blocks) // CORES
    if share % LANES:
        flat = kernel[:, 0, :]
        parts = [lax.dynamic_slice_in_dim(flat, b * share, share, 1) for b in blocks]
        return [jnp.concatenate(parts[i * CORES : (i + 1) * CORES], axis=1) for i in range(count)]
    return pl.pallas_call(
        pick_body,
        in_specs=[
            pl.BlockSpec(memory_space=pltpu.SMEM),
            pl.BlockSpec(memory_space=pltpu.VMEM),
        ],
        out_specs=[pl.BlockSpec(memory_space=pltpu.VMEM)] * count,
        out_shape=[jax.ShapeDtypeStruct((rows, CORES * share), jnp.float32)] * count,
        compiler_params=pltpu.CompilerParams(vmem_limit_bytes=16 * MIB),
        cost_estimate=pl.CostEstimate(flops=0, bytes_accessed=4 * kernel.size, transcendentals=0),
    )(jnp.stack(blocks).astype(jnp.int32), kernel)


def per_device(orbitals, kernel):
    nchips = lax.axis_size("blk") // CORES
    nshares = lax.axis_size("split")
    q = lax.axis_index("blk")
    share_id = lax.axis_index("split")
    chip = q // CORES
    share = orbitals.shape[0] // nshares
    half, near = nchips // 2, nchips // 4
    across = half ^ near

    def is_inner(c):
        return (c // half) != (c // near) % 2

    inner_chips = [c for c in range(nchips) if is_inner(c)]
    outer_chips = [c for c in range(nchips) if not is_inner(c)]
    inner = (chip // half) != (chip // near) % 2

    def along(value, pairs):
        full = [(CORES * a + c, CORES * b + c) for a, b in pairs for c in range(CORES)]
        return lax.ppermute(value, "blk", full)

    def other_core(value):
        return lax.ppermute(value, "blk", [(i, i ^ 1) for i in range(nchips * CORES)])

    own = lax.dynamic_slice_in_dim(orbitals, share_id * share, share, 0)
    pair_own = other_core(own)
    x = along(own, [(c, c ^ half) for c in outer_chips] + [(c, c ^ near) for c in inner_chips])

    others = [k for k in range(1, nchips) if k not in (near, half, across)]
    blocks = []
    for k in [0, jnp.where(inner, half, near), across] + others:
        blocks += [q ^ (CORES * k), q ^ (CORES * k + 1)]
    z_own, z_x, z_late, *z_others = pick_columns(kernel, blocks, share)

    def weighted(z_part, points):
        return z_part * product(orbitals, points, ((1,), (1,)))

    def rows_of(weights, points):
        return product(weights, points, ((1,), (0,)))

    points = jnp.concatenate([own, pair_own], axis=0)
    total = rows_of(weighted(z_own, points), points)

    own_late, z_x, z_late = lax.optimization_barrier((own, z_x, z_late))
    swapped = along(own_late, [(c, c ^ across) for c in inner_chips])

    for k, z_k in zip(others, z_others):
        more = along(own_late, [(c, c ^ k) for c in range(nchips)])
        points = jnp.concatenate([more, other_core(more)], axis=0)
        total += rows_of(weighted(z_k, points), points)

    passed = along(x, [(c, c ^ near) for c in range(nchips)])
    points = jnp.concatenate([x, other_core(x)], axis=0)
    weights = weighted(z_x, points)
    back = product(weights, orbitals, ((0,), (0,)))
    back = back[:share] + other_core(back[share:])
    total += rows_of(weights, points)

    total, back, passed, swapped = lax.optimization_barrier((total, back, passed, swapped))
    held = jnp.where(inner, swapped, passed)
    pair_held = other_core(held)
    z_last = z_late
    total += rows_of(weighted(z_last[:, :share], held), held)
    total, pair_held = lax.optimization_barrier((total, pair_held))
    total += rows_of(weighted(z_last[:, share:], pair_held), pair_held)
    total, back = lax.optimization_barrier((total, back))
    returned = along(
        back, [(c, c ^ half) for c in inner_chips] + [(c, c ^ near) for c in outer_chips]
    )

    bits = nshares.bit_length() - 1

    def bit_at(step, on_core):
        return (step + on_core * (bits // 2)) % bits

    def share_mask(place, on_core):
        return sum(((place >> (bits - 1 - t)) & 1) << bit_at(t, on_core) for t in range(bits))

    masks = [jnp.where(q % CORES == 0, share_mask(p, 0), share_mask(p, 1)) for p in range(nshares)]
    cut = orbitals.shape[1] // CHUNKS

    def blocks_of(places, chunk):
        found = [
            lax.dynamic_slice(total, ((share_id ^ masks[p]) * share, chunk * cut), (share, cut))
            for p in places
        ]
        return jnp.concatenate(found, axis=0)

    def halve(keep, send, step):
        pairs = [
            (b * nshares + s, b * nshares + (s ^ (1 << bit_at(step, b % CORES))))
            for b in range(nchips * CORES)
            for s in range(nshares)
        ]
        return keep + lax.ppermute(send, ("blk", "split"), pairs)

    places, middle = list(range(nshares)), nshares // 2
    parts = [halve(blocks_of(places[:middle], k), blocks_of(places[middle:], k), 0) for k in range(CHUNKS)]
    for step in range(1, bits):
        size = parts[0].shape[0] // 2
        parts = [halve(part[:size], part[size:], step) for part in parts]
    return jnp.concatenate(parts, axis=1) + returned


def solution(mesh):
    placed = (P("blk", None), P("blk", "split", None))
    return jax.shard_map(
        per_device, mesh=mesh, in_specs=placed, out_specs=P(("blk", "split"), None), check_vma=False
    )
```

```python
import jax
import jax.numpy as jnp
from jax import lax
from jax.experimental import pallas as pl
from jax.experimental.pallas import tpu as pltpu
from jax.sharding import PartitionSpec as P

CORES = 2
CHUNKS = 2
LANES = 128
MIB = 1 << 20


def product(a, b, dims):
    return lax.dot_general(
        a, b, (dims, ((), ())), precision=lax.Precision.HIGH, preferred_element_type=jnp.float32
    )


def pick_body(at_ref, kernel_ref, *out_refs):
    share = out_refs[0].shape[1] // CORES
    for i, out_ref in enumerate(out_refs):
        for c in range(CORES):
            start = pl.multiple_of(at_ref[i * CORES + c] * share, share)
            out_ref[:, c * share : (c + 1) * share] = kernel_ref[:, 0, pl.ds(start, share)]


def pick_columns(kernel, blocks, share):
    rows, count = kernel.shape[0], len(blocks) // CORES
    if share % LANES:
        flat = kernel[:, 0, :]
        parts = [lax.dynamic_slice_in_dim(flat, b * share, share, 1) for b in blocks]
        return [jnp.concatenate(parts[i * CORES : (i + 1) * CORES], axis=1) for i in range(count)]
    return pl.pallas_call(
        pick_body,
        in_specs=[
            pl.BlockSpec(memory_space=pltpu.SMEM),
            pl.BlockSpec(memory_space=pltpu.VMEM),
        ],
        out_specs=[pl.BlockSpec(memory_space=pltpu.VMEM)] * count,
        out_shape=[jax.ShapeDtypeStruct((rows, CORES * share), jnp.float32)] * count,
        compiler_params=pltpu.CompilerParams(vmem_limit_bytes=16 * MIB),
        cost_estimate=pl.CostEstimate(flops=0, bytes_accessed=4 * kernel.size, transcendentals=0),
    )(jnp.stack(blocks).astype(jnp.int32), kernel)


def per_device(orbitals, kernel):
    nchips = lax.axis_size("blk") // CORES
    nshares = lax.axis_size("split")
    q = lax.axis_index("blk")
    share_id = lax.axis_index("split")
    chip = q // CORES
    share = orbitals.shape[0] // nshares
    half, near = nchips // 2, nchips // 4
    across = half ^ near

    def is_inner(c):
        return (c // half) != (c // near) % 2

    inner_chips = [c for c in range(nchips) if is_inner(c)]
    outer_chips = [c for c in range(nchips) if not is_inner(c)]
    inner = (chip // half) != (chip // near) % 2

    def along(value, pairs):
        full = [(CORES * a + c, CORES * b + c) for a, b in pairs for c in range(CORES)]
        return lax.ppermute(value, "blk", full)

    def other_core(value):
        return lax.ppermute(value, "blk", [(i, i ^ 1) for i in range(nchips * CORES)])

    own = lax.dynamic_slice_in_dim(orbitals, share_id * share, share, 0)
    pair_own = other_core(own)
    x = along(own, [(c, c ^ half) for c in outer_chips] + [(c, c ^ near) for c in inner_chips])

    others = [k for k in range(1, nchips) if k not in (near, half, across)]
    blocks = []
    for k in [0, jnp.where(inner, half, near), across] + others:
        blocks += [q ^ (CORES * k), q ^ (CORES * k + 1)]
    z_own, z_x, z_late, *z_others = pick_columns(kernel, blocks, share)

    def weighted(z_part, points):
        return z_part * product(orbitals, points, ((1,), (1,)))

    def rows_of(weights, points):
        return product(weights, points, ((1,), (0,)))

    points = jnp.concatenate([own, pair_own], axis=0)
    total = rows_of(weighted(z_own, points), points)

    own_late, z_x, z_late = lax.optimization_barrier((own, z_x, z_late))
    swapped = along(own_late, [(c, c ^ across) for c in inner_chips])

    for k, z_k in zip(others, z_others):
        more = along(own_late, [(c, c ^ k) for c in range(nchips)])
        points = jnp.concatenate([more, other_core(more)], axis=0)
        total += rows_of(weighted(z_k, points), points)

    passed = along(x, [(c, c ^ near) for c in range(nchips)])
    points = jnp.concatenate([x, other_core(x)], axis=0)
    weights = weighted(z_x, points)
    back = product(weights, orbitals, ((0,), (0,)))
    back = back[:share] + other_core(back[share:])
    total += rows_of(weights, points)

    total, back, swapped = lax.optimization_barrier((total, back, swapped))
    swapped = jnp.where(inner, swapped, own)
    total, back, passed, swapped = lax.optimization_barrier((total, back, passed, swapped))
    held = jnp.where(inner, swapped, passed)
    pair_held = other_core(held)
    z_last = z_late
    total += rows_of(weighted(z_last[:, :share], held), held)
    total, pair_held = lax.optimization_barrier((total, pair_held))
    last = rows_of(weighted(z_last[:, share:], pair_held), pair_held)
    total, last, back = lax.optimization_barrier((total, last, back))
    returned = along(
        back, [(c, c ^ half) for c in inner_chips] + [(c, c ^ near) for c in outer_chips]
    )

    bits = nshares.bit_length() - 1

    def bit_at(step, on_core):
        return (step + on_core * (bits // 2)) % bits

    def share_mask(place, on_core):
        return sum(((place >> (bits - 1 - t)) & 1) << bit_at(t, on_core) for t in range(bits))

    masks = [jnp.where(q % CORES == 0, share_mask(p, 0), share_mask(p, 1)) for p in range(nshares)]
    cut = orbitals.shape[1] // CHUNKS

    def block_of(value, place, chunk):
        start = ((share_id ^ masks[place]) * share, chunk * cut)
        return lax.dynamic_slice(value, start, (share, cut))

    def blocks_of(places, chunk):
        found = [block_of(total, p, chunk) + block_of(last, p, chunk) for p in places]
        return jnp.concatenate(found, axis=0)

    def halve(keep, send, step):
        pairs = [
            (b * nshares + s, b * nshares + (s ^ (1 << bit_at(step, b % CORES))))
            for b in range(nchips * CORES)
            for s in range(nshares)
        ]
        return keep + lax.ppermute(send, ("blk", "split"), pairs)

    places, middle = list(range(nshares)), nshares // 2
    parts = [halve(blocks_of(places[:middle], k), blocks_of(places[middle:], k), 0) for k in range(CHUNKS)]
    for step in range(1, bits):
        size = parts[0].shape[0] // 2
        parts = [halve(part[:size], part[size:], step) for part in parts]
    return jnp.concatenate(parts, axis=1) + returned


def solution(mesh):
    placed = (P("blk", None), P("blk", "split", None))
    return jax.shard_map(
        per_device, mesh=mesh, in_specs=placed, out_specs=P(("blk", "split"), None), check_vma=False
    )
```

```python
import jax
import jax.numpy as jnp
from jax import lax
from jax.experimental import pallas as pl
from jax.experimental.pallas import tpu as pltpu
from jax.sharding import PartitionSpec as P

CORES = 2
CHUNKS = 2
LANES = 128
MIB = 1 << 20


def product(a, b, dims):
    return lax.dot_general(
        a, b, (dims, ((), ())), precision=lax.Precision.HIGH, preferred_element_type=jnp.float32
    )


def pick_body(at_ref, kernel_ref, *out_refs):
    share = out_refs[0].shape[1] // CORES
    for i, out_ref in enumerate(out_refs):
        for c in range(CORES):
            start = pl.multiple_of(at_ref[i * CORES + c] * share, share)
            out_ref[:, c * share : (c + 1) * share] = kernel_ref[:, 0, pl.ds(start, share)]


def pick_columns(kernel, blocks, share):
    rows, count = kernel.shape[0], len(blocks) // CORES
    if share % LANES:
        flat = kernel[:, 0, :]
        parts = [lax.dynamic_slice_in_dim(flat, b * share, share, 1) for b in blocks]
        return [jnp.concatenate(parts[i * CORES : (i + 1) * CORES], axis=1) for i in range(count)]
    return pl.pallas_call(
        pick_body,
        in_specs=[
            pl.BlockSpec(memory_space=pltpu.SMEM),
            pl.BlockSpec(memory_space=pltpu.VMEM),
        ],
        out_specs=[pl.BlockSpec(memory_space=pltpu.VMEM)] * count,
        out_shape=[jax.ShapeDtypeStruct((rows, CORES * share), jnp.float32)] * count,
        compiler_params=pltpu.CompilerParams(vmem_limit_bytes=16 * MIB),
        cost_estimate=pl.CostEstimate(flops=0, bytes_accessed=4 * kernel.size, transcendentals=0),
    )(jnp.stack(blocks).astype(jnp.int32), kernel)


def per_device(orbitals, kernel):
    nchips = lax.axis_size("blk") // CORES
    nshares = lax.axis_size("split")
    q = lax.axis_index("blk")
    share_id = lax.axis_index("split")
    chip = q // CORES
    share = orbitals.shape[0] // nshares
    half, near = nchips // 2, nchips // 4
    across = half ^ near

    def is_inner(c):
        return (c // half) != (c // near) % 2

    inner_chips = [c for c in range(nchips) if is_inner(c)]
    outer_chips = [c for c in range(nchips) if not is_inner(c)]
    inner = (chip // half) != (chip // near) % 2

    def along(value, pairs):
        full = [(CORES * a + c, CORES * b + c) for a, b in pairs for c in range(CORES)]
        return lax.ppermute(value, "blk", full)

    def other_core(value):
        return lax.ppermute(value, "blk", [(i, i ^ 1) for i in range(nchips * CORES)])

    own = lax.dynamic_slice_in_dim(orbitals, share_id * share, share, 0)
    pair_own = other_core(own)
    x = along(own, [(c, c ^ half) for c in outer_chips] + [(c, c ^ near) for c in inner_chips])

    others = [k for k in range(1, nchips) if k not in (near, half, across)]
    blocks = []
    for k in [0, jnp.where(inner, half, near), across] + others:
        blocks += [q ^ (CORES * k), q ^ (CORES * k + 1)]
    z_own, z_x, z_late, *z_others = pick_columns(kernel, blocks, share)

    def weighted(z_part, points):
        return z_part * product(orbitals, points, ((1,), (1,)))

    def rows_of(weights, points):
        return product(weights, points, ((1,), (0,)))

    points = jnp.concatenate([own, pair_own], axis=0)
    total = rows_of(weighted(z_own, points), points)

    own_late, z_x, z_late = lax.optimization_barrier((own, z_x, z_late))
    swapped = along(own_late, [(c, c ^ across) for c in inner_chips])

    for k, z_k in zip(others, z_others):
        more = along(own_late, [(c, c ^ k) for c in range(nchips)])
        points = jnp.concatenate([more, other_core(more)], axis=0)
        total += rows_of(weighted(z_k, points), points)

    passed = along(x, [(c, c ^ near) for c in range(nchips)])
    points = jnp.concatenate([x, other_core(x)], axis=0)
    weights = weighted(z_x, points)
    back = product(weights, orbitals, ((0,), (0,)))
    back = back[:share] + other_core(back[share:])
    total += rows_of(weights, points)

    total, back, swapped = lax.optimization_barrier((total, back, swapped))
    swapped = jnp.where(inner, swapped, own)
    total, back, passed, swapped = lax.optimization_barrier((total, back, passed, swapped))
    held = jnp.where(inner, swapped, passed)
    pair_held = other_core(held)
    z_last = z_late
    total += rows_of(weighted(z_last[:, :share], held), held)
    total, pair_held = lax.optimization_barrier((total, pair_held))
    last = rows_of(weighted(z_last[:, share:], pair_held), pair_held)
    total, last, back = lax.optimization_barrier((total, last, back))
    returned = along(
        back, [(c, c ^ half) for c in inner_chips] + [(c, c ^ near) for c in outer_chips]
    )

    bits = nshares.bit_length() - 1

    def bit_at(step, on_core):
        return (step + on_core * (bits // 2)) % bits

    def share_mask(place, on_core):
        return sum(((place >> (bits - 1 - t)) & 1) << bit_at(t, on_core) for t in range(bits))

    masks = [jnp.where(q % CORES == 0, share_mask(p, 0), share_mask(p, 1)) for p in range(nshares)]
    cut = orbitals.shape[1] * 1 // 2
    cuts = [(0, cut), (cut, orbitals.shape[1] - cut)]

    def block_of(value, place, start, size):
        start = ((share_id ^ masks[place]) * share, start)
        return lax.dynamic_slice(value, start, (share, size))

    def blocks_of(places, where):
        found = [block_of(total, p, *where) + block_of(last, p, *where) for p in places]
        return jnp.concatenate(found, axis=0)

    def exchange(send, step):
        pairs = [
            (b * nshares + s, b * nshares + (s ^ (1 << bit_at(step, b % CORES))))
            for b in range(nchips * CORES)
            for s in range(nshares)
        ]
        return lax.ppermute(send, ("blk", "split"), pairs)

    places, middle = list(range(nshares)), nshares // 2
    gots = [exchange(blocks_of(places[middle:], where), 0) for where in cuts]
    wide = blocks_of(places[:middle], cuts[0]) + gots[0]
    got, _ = lax.optimization_barrier((gots[1], wide))
    parts = [wide, blocks_of(places[:middle], cuts[1]) + got]
    for step in range(1, bits):
        size = parts[0].shape[0] // 2
        parts = [part[:size] + exchange(part[size:], step) for part in parts]
    return jnp.concatenate(parts, axis=1) + returned


def solution(mesh):
    placed = (P("blk", None), P("blk", "split", None))
    return jax.shard_map(
        per_device, mesh=mesh, in_specs=placed, out_specs=P(("blk", "split"), None), check_vma=False
    )
```

```python
import jax
import jax.numpy as jnp
from jax import lax
from jax.experimental import pallas as pl
from jax.experimental.pallas import tpu as pltpu
from jax.sharding import PartitionSpec as P

CORES = 2
CHUNKS = 2
LANES = 128
MIB = 1 << 20


def product(a, b, dims):
    return lax.dot_general(
        a, b, (dims, ((), ())), precision=lax.Precision.HIGH, preferred_element_type=jnp.float32
    )


def split(value):
    high = lax.reduce_precision(value, exponent_bits=8, mantissa_bits=7)
    return high.astype(jnp.bfloat16), (value - high).astype(jnp.bfloat16)


def single(a, b, dims):
    return lax.dot_general(a, b, (dims, ((), ())), preferred_element_type=jnp.float32)


def pick_body(at_ref, kernel_ref, *out_refs):
    share = out_refs[0].shape[1] // CORES
    for i, out_ref in enumerate(out_refs):
        for c in range(CORES):
            start = pl.multiple_of(at_ref[i * CORES + c] * share, share)
            out_ref[:, c * share : (c + 1) * share] = kernel_ref[:, 0, pl.ds(start, share)]


def pick_columns(kernel, blocks, share):
    rows, count = kernel.shape[0], len(blocks) // CORES
    if share % LANES:
        flat = kernel[:, 0, :]
        parts = [lax.dynamic_slice_in_dim(flat, b * share, share, 1) for b in blocks]
        return [jnp.concatenate(parts[i * CORES : (i + 1) * CORES], axis=1) for i in range(count)]
    return pl.pallas_call(
        pick_body,
        in_specs=[
            pl.BlockSpec(memory_space=pltpu.SMEM),
            pl.BlockSpec(memory_space=pltpu.VMEM),
        ],
        out_specs=[pl.BlockSpec(memory_space=pltpu.VMEM)] * count,
        out_shape=[jax.ShapeDtypeStruct((rows, CORES * share), jnp.float32)] * count,
        compiler_params=pltpu.CompilerParams(vmem_limit_bytes=16 * MIB),
        cost_estimate=pl.CostEstimate(flops=0, bytes_accessed=4 * kernel.size, transcendentals=0),
    )(jnp.stack(blocks).astype(jnp.int32), kernel)


def per_device(orbitals, kernel):
    nchips = lax.axis_size("blk") // CORES
    nshares = lax.axis_size("split")
    q = lax.axis_index("blk")
    share_id = lax.axis_index("split")
    chip = q // CORES
    share = orbitals.shape[0] // nshares
    half, near = nchips // 2, nchips // 4
    across = half ^ near

    def is_inner(c):
        return (c // half) != (c // near) % 2

    inner_chips = [c for c in range(nchips) if is_inner(c)]
    outer_chips = [c for c in range(nchips) if not is_inner(c)]
    inner = (chip // half) != (chip // near) % 2

    def along(value, pairs):
        full = [(CORES * a + c, CORES * b + c) for a, b in pairs for c in range(CORES)]
        return lax.ppermute(value, "blk", full)

    def other_core(value):
        return lax.ppermute(value, "blk", [(i, i ^ 1) for i in range(nchips * CORES)])

    own = lax.dynamic_slice_in_dim(orbitals, share_id * share, share, 0)
    pair_own = other_core(own)
    x = along(own, [(c, c ^ half) for c in outer_chips] + [(c, c ^ near) for c in inner_chips])

    others = [k for k in range(1, nchips) if k not in (near, half, across)]
    blocks = []
    for k in [0, jnp.where(inner, half, near), across] + others:
        blocks += [q ^ (CORES * k), q ^ (CORES * k + 1)]
    z_own, z_x, z_late, *z_others = pick_columns(kernel, blocks, share)

    def weighted(z_part, points):
        return z_part * product(orbitals, points, ((1,), (1,)))

    def rows_of(weights, points):
        return product(weights, points, ((1,), (0,)))

    points = jnp.concatenate([own, pair_own], axis=0)
    total = rows_of(weighted(z_own, points), points)

    own_late, z_x, z_late = lax.optimization_barrier((own, z_x, z_late))
    swapped = along(own_late, [(c, c ^ across) for c in inner_chips])

    for k, z_k in zip(others, z_others):
        more = along(own_late, [(c, c ^ k) for c in range(nchips)])
        points = jnp.concatenate([more, other_core(more)], axis=0)
        total += rows_of(weighted(z_k, points), points)

    passed = along(x, [(c, c ^ near) for c in range(nchips)])
    points = jnp.concatenate([x, other_core(x)], axis=0)
    weights = weighted(z_x, points)
    back = product(weights, orbitals, ((0,), (0,)))
    back = back[:share] + other_core(back[share:])
    total += rows_of(weights, points)

    total, back, swapped = lax.optimization_barrier((total, back, swapped))
    swapped = jnp.where(inner, swapped, own)
    total, back, passed, swapped = lax.optimization_barrier((total, back, passed, swapped))
    held = jnp.where(inner, swapped, passed)
    pair_held = other_core(held)
    z_last = z_late
    total += rows_of(weighted(z_last[:, :share], held), held)
    total, pair_held = lax.optimization_barrier((total, pair_held))
    high, low = split(pair_held)
    w_high, w_low = split(weighted(z_last[:, share:], pair_held))
    last = single(
        jnp.concatenate([w_high, w_low, w_high], axis=1),
        jnp.concatenate([high, high, low], axis=0),
        ((1,), (0,)),
    )
    total, last, back = lax.optimization_barrier((total, last, back))
    returned = along(
        back, [(c, c ^ half) for c in inner_chips] + [(c, c ^ near) for c in outer_chips]
    )

    bits = nshares.bit_length() - 1

    def bit_at(step, on_core):
        return (step + on_core * (bits // 2)) % bits

    def share_mask(place, on_core):
        return sum(((place >> (bits - 1 - t)) & 1) << bit_at(t, on_core) for t in range(bits))

    masks = [jnp.where(q % CORES == 0, share_mask(p, 0), share_mask(p, 1)) for p in range(nshares)]
    cut = orbitals.shape[1] // 2
    cuts = [(0, cut), (cut, orbitals.shape[1] - cut)]

    def block_of(value, place, start, size):
        start = ((share_id ^ masks[place]) * share, start)
        return lax.dynamic_slice(value, start, (share, size))

    def blocks_of(places, where):
        found = [block_of(total, p, *where) + block_of(last, p, *where) for p in places]
        return jnp.concatenate(found, axis=0)

    def exchange(send, step):
        pairs = [
            (b * nshares + s, b * nshares + (s ^ (1 << bit_at(step, b % CORES))))
            for b in range(nchips * CORES)
            for s in range(nshares)
        ]
        return lax.ppermute(send, ("blk", "split"), pairs)

    places, middle = list(range(nshares)), nshares // 2
    gots = [exchange(blocks_of(places[middle:], where), 0) for where in cuts]
    wide = blocks_of(places[:middle], cuts[0]) + gots[0]
    got, _ = lax.optimization_barrier((gots[1], wide))
    parts = [wide, blocks_of(places[:middle], cuts[1]) + got]
    for step in range(1, bits):
        size = parts[0].shape[0] // 2
        parts = [part[:size] + exchange(part[size:], step) for part in parts]
    return jnp.concatenate(parts, axis=1) + returned


def solution(mesh):
    placed = (P("blk", None), P("blk", "split", None))
    return jax.shard_map(
        per_device, mesh=mesh, in_specs=placed, out_specs=P(("blk", "split"), None), check_vma=False
    )
```

```python
import jax
import jax.numpy as jnp
from jax import lax
from jax.experimental import pallas as pl
from jax.experimental.pallas import tpu as pltpu
from jax.sharding import PartitionSpec as P

CORES = 2
CHUNKS = 2
LANES = 128
MIB = 1 << 20


def product(a, b, dims):
    return lax.dot_general(
        a, b, (dims, ((), ())), precision=lax.Precision.HIGH, preferred_element_type=jnp.float32
    )


def pick_body(at_ref, kernel_ref, *out_refs):
    share = out_refs[0].shape[1] // CORES
    for i, out_ref in enumerate(out_refs):
        for c in range(CORES):
            start = pl.multiple_of(at_ref[i * CORES + c] * share, share)
            out_ref[:, c * share : (c + 1) * share] = kernel_ref[:, 0, pl.ds(start, share)]


def pick_columns(kernel, blocks, share):
    rows, count = kernel.shape[0], len(blocks) // CORES
    if share % LANES:
        flat = kernel[:, 0, :]
        parts = [lax.dynamic_slice_in_dim(flat, b * share, share, 1) for b in blocks]
        return [jnp.concatenate(parts[i * CORES : (i + 1) * CORES], axis=1) for i in range(count)]
    return pl.pallas_call(
        pick_body,
        in_specs=[
            pl.BlockSpec(memory_space=pltpu.SMEM),
            pl.BlockSpec(memory_space=pltpu.VMEM),
        ],
        out_specs=[pl.BlockSpec(memory_space=pltpu.VMEM)] * count,
        out_shape=[jax.ShapeDtypeStruct((rows, CORES * share), jnp.float32)] * count,
        compiler_params=pltpu.CompilerParams(vmem_limit_bytes=16 * MIB),
        cost_estimate=pl.CostEstimate(flops=0, bytes_accessed=4 * kernel.size, transcendentals=0),
    )(jnp.stack(blocks).astype(jnp.int32), kernel)


def per_device(orbitals, kernel):
    nchips = lax.axis_size("blk") // CORES
    nshares = lax.axis_size("split")
    q = lax.axis_index("blk")
    share_id = lax.axis_index("split")
    chip = q // CORES
    share = orbitals.shape[0] // nshares
    half, near = nchips // 2, nchips // 4
    across = half ^ near

    def is_inner(c):
        return (c // half) != (c // near) % 2

    inner_chips = [c for c in range(nchips) if is_inner(c)]
    outer_chips = [c for c in range(nchips) if not is_inner(c)]
    inner = (chip // half) != (chip // near) % 2

    def along(value, pairs):
        full = [(CORES * a + c, CORES * b + c) for a, b in pairs for c in range(CORES)]
        return lax.ppermute(value, "blk", full)

    def other_core(value):
        return lax.ppermute(value, "blk", [(i, i ^ 1) for i in range(nchips * CORES)])

    own = lax.dynamic_slice_in_dim(orbitals, share_id * share, share, 0)
    pair_own = other_core(own)
    x = along(own, [(c, c ^ half) for c in outer_chips] + [(c, c ^ near) for c in inner_chips])

    others = [k for k in range(1, nchips) if k not in (near, half, across)]
    blocks = []
    for k in [0, jnp.where(inner, half, near), across] + others:
        blocks += [q ^ (CORES * k), q ^ (CORES * k + 1)]
    z_own, z_x, z_late, *z_others = pick_columns(kernel, blocks, share)

    def weighted(z_part, points):
        return z_part * product(orbitals, points, ((1,), (1,)))

    def rows_of(weights, points):
        return product(weights, points, ((1,), (0,)))

    points = jnp.concatenate([own, pair_own], axis=0)
    total = rows_of(weighted(z_own, points), points)

    own_late, z_x, z_late = lax.optimization_barrier((own, z_x, z_late))
    swapped = along(own_late, [(c, c ^ across) for c in inner_chips])

    for k, z_k in zip(others, z_others):
        more = along(own_late, [(c, c ^ k) for c in range(nchips)])
        points = jnp.concatenate([more, other_core(more)], axis=0)
        total += rows_of(weighted(z_k, points), points)

    passed = along(x, [(c, c ^ near) for c in range(nchips)])
    points = jnp.concatenate([x, other_core(x)], axis=0)
    weights = weighted(z_x, points)
    back = product(weights, orbitals, ((0,), (0,)))
    back = back[:share] + other_core(back[share:])
    total += rows_of(weights, points)

    total, back, swapped = lax.optimization_barrier((total, back, swapped))
    swapped = jnp.where(inner, swapped, own)
    total, back, passed, swapped = lax.optimization_barrier((total, back, passed, swapped))
    held = jnp.where(inner, swapped, passed)
    pair_held = other_core(held)
    z_last = z_late
    total += rows_of(weighted(z_last[:, :share], held), held)
    total, pair_held = lax.optimization_barrier((total, pair_held))
    last = rows_of(weighted(z_last[:, share:], pair_held), pair_held)
    total, last = lax.optimization_barrier((total, last))
    returned = along(
        back, [(c, c ^ half) for c in inner_chips] + [(c, c ^ near) for c in outer_chips]
    )

    bits = nshares.bit_length() - 1

    def bit_at(step, on_core):
        return (step + on_core * (bits // 2)) % bits

    def share_mask(place, on_core):
        return sum(((place >> (bits - 1 - t)) & 1) << bit_at(t, on_core) for t in range(bits))

    masks = [jnp.where(q % CORES == 0, share_mask(p, 0), share_mask(p, 1)) for p in range(nshares)]
    cut = orbitals.shape[1] // 2
    cuts = [(0, cut), (cut, orbitals.shape[1] - cut)]

    def block_of(value, place, start, size):
        start = ((share_id ^ masks[place]) * share, start)
        return lax.dynamic_slice(value, start, (share, size))

    def blocks_of(places, where):
        found = [block_of(total, p, *where) + block_of(last, p, *where) for p in places]
        return jnp.concatenate(found, axis=0)

    def exchange(send, step):
        pairs = [
            (b * nshares + s, b * nshares + (s ^ (1 << bit_at(step, b % CORES))))
            for b in range(nchips * CORES)
            for s in range(nshares)
        ]
        return lax.ppermute(send, ("blk", "split"), pairs)

    places, middle = list(range(nshares)), nshares // 2
    gots = [exchange(blocks_of(places[middle:], where), 0) for where in cuts]
    wide = blocks_of(places[:middle], cuts[0]) + gots[0]
    got, _ = lax.optimization_barrier((gots[1], wide))
    parts = [wide, blocks_of(places[:middle], cuts[1]) + got]
    for step in range(1, bits):
        size = parts[0].shape[0] // 2
        parts = [part[:size] + exchange(part[size:], step) for part in parts]
    return jnp.concatenate(parts, axis=1) + returned


def solution(mesh):
    placed = (P("blk", None), P("blk", "split", None))
    return jax.shard_map(
        per_device, mesh=mesh, in_specs=placed, out_specs=P(("blk", "split"), None), check_vma=False
    )
```

```python
import jax
import jax.numpy as jnp
from jax import lax
from jax.experimental import pallas as pl
from jax.experimental.pallas import tpu as pltpu
from jax.sharding import PartitionSpec as P

CORES = 2
CHUNKS = 2
LANES = 128
MIB = 1 << 20


def product(a, b, dims):
    return lax.dot_general(
        a, b, (dims, ((), ())), precision=lax.Precision.HIGH, preferred_element_type=jnp.float32
    )


def split(value):
    high = lax.reduce_precision(value, exponent_bits=8, mantissa_bits=7)
    return high.astype(jnp.bfloat16), (value - high).astype(jnp.bfloat16)


def single(a, b, dims):
    return lax.dot_general(a, b, (dims, ((), ())), preferred_element_type=jnp.float32)


def pick_body(at_ref, kernel_ref, *out_refs):
    share = out_refs[0].shape[1] // CORES
    for i, out_ref in enumerate(out_refs):
        for c in range(CORES):
            start = pl.multiple_of(at_ref[i * CORES + c] * share, share)
            out_ref[:, c * share : (c + 1) * share] = kernel_ref[:, 0, pl.ds(start, share)]


def pick_columns(kernel, blocks, share):
    rows, count = kernel.shape[0], len(blocks) // CORES
    if share % LANES:
        flat = kernel[:, 0, :]
        parts = [lax.dynamic_slice_in_dim(flat, b * share, share, 1) for b in blocks]
        return [jnp.concatenate(parts[i * CORES : (i + 1) * CORES], axis=1) for i in range(count)]
    return pl.pallas_call(
        pick_body,
        in_specs=[
            pl.BlockSpec(memory_space=pltpu.SMEM),
            pl.BlockSpec(memory_space=pltpu.VMEM),
        ],
        out_specs=[pl.BlockSpec(memory_space=pltpu.VMEM)] * count,
        out_shape=[jax.ShapeDtypeStruct((rows, CORES * share), jnp.float32)] * count,
        compiler_params=pltpu.CompilerParams(vmem_limit_bytes=16 * MIB),
        cost_estimate=pl.CostEstimate(flops=0, bytes_accessed=4 * kernel.size, transcendentals=0),
    )(jnp.stack(blocks).astype(jnp.int32), kernel)


def per_device(orbitals, kernel):
    nchips = lax.axis_size("blk") // CORES
    nshares = lax.axis_size("split")
    q = lax.axis_index("blk")
    share_id = lax.axis_index("split")
    chip = q // CORES
    share = orbitals.shape[0] // nshares
    half, near = nchips // 2, nchips // 4
    across = half ^ near

    def is_inner(c):
        return (c // half) != (c // near) % 2

    inner_chips = [c for c in range(nchips) if is_inner(c)]
    outer_chips = [c for c in range(nchips) if not is_inner(c)]
    inner = (chip // half) != (chip // near) % 2

    def along(value, pairs):
        full = [(CORES * a + c, CORES * b + c) for a, b in pairs for c in range(CORES)]
        return lax.ppermute(value, "blk", full)

    def other_core(value):
        return lax.ppermute(value, "blk", [(i, i ^ 1) for i in range(nchips * CORES)])

    own = lax.dynamic_slice_in_dim(orbitals, share_id * share, share, 0)
    pair_own = other_core(own)
    x = along(own, [(c, c ^ half) for c in outer_chips] + [(c, c ^ near) for c in inner_chips])

    others = [k for k in range(1, nchips) if k not in (near, half, across)]
    blocks = []
    for k in [0, jnp.where(inner, half, near), across] + others:
        blocks += [q ^ (CORES * k), q ^ (CORES * k + 1)]
    z_own, z_x, z_late, *z_others = pick_columns(kernel, blocks, share)

    def weighted(z_part, points):
        return z_part * product(orbitals, points, ((1,), (1,)))

    def rows_of(weights, points):
        return product(weights, points, ((1,), (0,)))

    points = jnp.concatenate([own, pair_own], axis=0)
    total = rows_of(weighted(z_own, points), points)

    own_late, z_x, z_late = lax.optimization_barrier((own, z_x, z_late))
    swapped = along(own_late, [(c, c ^ across) for c in inner_chips])

    for k, z_k in zip(others, z_others):
        more = along(own_late, [(c, c ^ k) for c in range(nchips)])
        points = jnp.concatenate([more, other_core(more)], axis=0)
        total += rows_of(weighted(z_k, points), points)

    passed = along(x, [(c, c ^ near) for c in range(nchips)])
    points = jnp.concatenate([x, other_core(x)], axis=0)
    weights = weighted(z_x, points)
    back = product(weights, orbitals, ((0,), (0,)))
    back = back[:share] + other_core(back[share:])
    total += rows_of(weights, points)

    total, back, swapped = lax.optimization_barrier((total, back, swapped))
    swapped = jnp.where(inner, swapped, own)
    total, back, passed, swapped = lax.optimization_barrier((total, back, passed, swapped))
    held = jnp.where(inner, swapped, passed)
    pair_held = other_core(held)
    z_last = z_late
    total += rows_of(weighted(z_last[:, :share], held), held)
    total, pair_held = lax.optimization_barrier((total, pair_held))
    high, low = split(pair_held)
    w_high, w_low = split(weighted(z_last[:, share:], pair_held))
    last = single(
        jnp.concatenate([w_high, w_low, w_high], axis=1),
        jnp.concatenate([high, high, low], axis=0),
        ((1,), (0,)),
    )
    total, last = lax.optimization_barrier((total, last))
    returned = along(
        back, [(c, c ^ half) for c in inner_chips] + [(c, c ^ near) for c in outer_chips]
    )

    bits = nshares.bit_length() - 1

    def bit_at(step, on_core):
        return (step + on_core * (bits // 2)) % bits

    def share_mask(place, on_core):
        return sum(((place >> (bits - 1 - t)) & 1) << bit_at(t, on_core) for t in range(bits))

    masks = [jnp.where(q % CORES == 0, share_mask(p, 0), share_mask(p, 1)) for p in range(nshares)]
    cut = orbitals.shape[1] // 2
    cuts = [(0, cut), (cut, orbitals.shape[1] - cut)]

    def block_of(value, place, start, size):
        start = ((share_id ^ masks[place]) * share, start)
        return lax.dynamic_slice(value, start, (share, size))

    def blocks_of(places, where):
        found = [block_of(total, p, *where) + block_of(last, p, *where) for p in places]
        return jnp.concatenate(found, axis=0)

    def exchange(send, step):
        pairs = [
            (b * nshares + s, b * nshares + (s ^ (1 << bit_at(step, b % CORES))))
            for b in range(nchips * CORES)
            for s in range(nshares)
        ]
        return lax.ppermute(send, ("blk", "split"), pairs)

    places, middle = list(range(nshares)), nshares // 2
    gots = [exchange(blocks_of(places[middle:], where), 0) for where in cuts]
    wide = blocks_of(places[:middle], cuts[0]) + gots[0]
    got, _ = lax.optimization_barrier((gots[1], wide))
    parts = [wide, blocks_of(places[:middle], cuts[1]) + got]
    for step in range(1, bits):
        size = parts[0].shape[0] // 2
        parts = [part[:size] + exchange(part[size:], step) for part in parts]
    return jnp.concatenate(parts, axis=1) + returned


def solution(mesh):
    placed = (P("blk", None), P("blk", "split", None))
    return jax.shard_map(
        per_device, mesh=mesh, in_specs=placed, out_specs=P(("blk", "split"), None), check_vma=False
    )
```

```python
import jax
import jax.numpy as jnp
from jax import lax
from jax.experimental import pallas as pl
from jax.experimental.pallas import tpu as pltpu
from jax.sharding import PartitionSpec as P

CORES = 2
CHUNKS = 2
LANES = 128
MIB = 1 << 20


def product(a, b, dims):
    return lax.dot_general(
        a, b, (dims, ((), ())), precision=lax.Precision.HIGH, preferred_element_type=jnp.float32
    )


def pick_body(at_ref, kernel_ref, *out_refs):
    share = out_refs[0].shape[1] // CORES
    for i, out_ref in enumerate(out_refs):
        for c in range(CORES):
            start = pl.multiple_of(at_ref[i * CORES + c] * share, share)
            out_ref[:, c * share : (c + 1) * share] = kernel_ref[:, 0, pl.ds(start, share)]


def pick_columns(kernel, blocks, share):
    rows, count = kernel.shape[0], len(blocks) // CORES
    if share % LANES:
        flat = kernel[:, 0, :]
        parts = [lax.dynamic_slice_in_dim(flat, b * share, share, 1) for b in blocks]
        return [jnp.concatenate(parts[i * CORES : (i + 1) * CORES], axis=1) for i in range(count)]
    return pl.pallas_call(
        pick_body,
        in_specs=[
            pl.BlockSpec(memory_space=pltpu.SMEM),
            pl.BlockSpec(memory_space=pltpu.VMEM),
        ],
        out_specs=[pl.BlockSpec(memory_space=pltpu.VMEM)] * count,
        out_shape=[jax.ShapeDtypeStruct((rows, CORES * share), jnp.float32)] * count,
        compiler_params=pltpu.CompilerParams(vmem_limit_bytes=16 * MIB),
        cost_estimate=pl.CostEstimate(flops=0, bytes_accessed=4 * kernel.size, transcendentals=0),
    )(jnp.stack(blocks).astype(jnp.int32), kernel)


def per_device(orbitals, kernel):
    nchips = lax.axis_size("blk") // CORES
    nshares = lax.axis_size("split")
    q = lax.axis_index("blk")
    share_id = lax.axis_index("split")
    chip = q // CORES
    share = orbitals.shape[0] // nshares
    half, near = nchips // 2, nchips // 4
    across = half ^ near

    def is_inner(c):
        return (c // half) != (c // near) % 2

    inner_chips = [c for c in range(nchips) if is_inner(c)]
    outer_chips = [c for c in range(nchips) if not is_inner(c)]
    inner = (chip // half) != (chip // near) % 2

    def along(value, pairs):
        full = [(CORES * a + c, CORES * b + c) for a, b in pairs for c in range(CORES)]
        return lax.ppermute(value, "blk", full)

    def other_core(value):
        return lax.ppermute(value, "blk", [(i, i ^ 1) for i in range(nchips * CORES)])

    own = lax.dynamic_slice_in_dim(orbitals, share_id * share, share, 0)
    pair_own = other_core(own)
    x = along(own, [(c, c ^ half) for c in outer_chips] + [(c, c ^ near) for c in inner_chips])

    others = [k for k in range(1, nchips) if k not in (near, half, across)]
    blocks = []
    for k in [0, jnp.where(inner, half, near), across] + others:
        blocks += [q ^ (CORES * k), q ^ (CORES * k + 1)]
    z_own, z_x, z_late, *z_others = pick_columns(kernel, blocks, share)

    def weighted(z_part, points):
        return z_part * product(orbitals, points, ((1,), (1,)))

    def rows_of(weights, points):
        return product(weights, points, ((1,), (0,)))

    points = jnp.concatenate([own, pair_own], axis=0)
    total = rows_of(weighted(z_own, points), points)

    own_late, z_x, z_late = lax.optimization_barrier((own, z_x, z_late))
    swapped = along(own_late, [(c, c ^ across) for c in inner_chips])

    for k, z_k in zip(others, z_others):
        more = along(own_late, [(c, c ^ k) for c in range(nchips)])
        points = jnp.concatenate([more, other_core(more)], axis=0)
        total += rows_of(weighted(z_k, points), points)

    passed = along(x, [(c, c ^ near) for c in range(nchips)])
    points = jnp.concatenate([x, other_core(x)], axis=0)
    weights = weighted(z_x, points)
    back = product(weights, orbitals, ((0,), (0,)))
    back = back[:share] + other_core(back[share:])
    total += rows_of(weights, points)

    total, back, swapped = lax.optimization_barrier((total, back, swapped))
    swapped = jnp.where(inner, swapped, own)
    total, back, passed, swapped = lax.optimization_barrier((total, back, passed, swapped))
    held = jnp.where(inner, swapped, passed)
    pair_held = other_core(held)
    z_last = z_late
    total += rows_of(weighted(z_last[:, :share], held), held)
    total, pair_held = lax.optimization_barrier((total, pair_held))
    last = rows_of(weighted(z_last[:, share:], pair_held), pair_held)
    total, last, back = lax.optimization_barrier((total, last, back))
    returned = along(
        back, [(c, c ^ half) for c in inner_chips] + [(c, c ^ near) for c in outer_chips]
    )

    bits = nshares.bit_length() - 1

    def bit_at(step, on_core):
        return (step + (1 - on_core) * (bits // 2)) % bits

    def share_mask(place, on_core):
        return sum(((place >> (bits - 1 - t)) & 1) << bit_at(t, on_core) for t in range(bits))

    masks = [jnp.where(q % CORES == 0, share_mask(p, 0), share_mask(p, 1)) for p in range(nshares)]
    cut = orbitals.shape[1] // 2
    cuts = [(0, cut), (cut, orbitals.shape[1] - cut)]

    def block_of(value, place, start, size):
        start = ((share_id ^ masks[place]) * share, start)
        return lax.dynamic_slice(value, start, (share, size))

    def blocks_of(places, where):
        found = [block_of(total, p, *where) + block_of(last, p, *where) for p in places]
        return jnp.concatenate(found, axis=0)

    def exchange(send, step):
        pairs = [
            (b * nshares + s, b * nshares + (s ^ (1 << bit_at(step, b % CORES))))
            for b in range(nchips * CORES)
            for s in range(nshares)
        ]
        return lax.ppermute(send, ("blk", "split"), pairs)

    places, middle = list(range(nshares)), nshares // 2
    gots = [exchange(blocks_of(places[middle:], where), 0) for where in cuts]
    wide = blocks_of(places[:middle], cuts[0]) + gots[0]
    got, _ = lax.optimization_barrier((gots[1], wide))
    parts = [wide, blocks_of(places[:middle], cuts[1]) + got]
    for step in range(1, bits):
        size = parts[0].shape[0] // 2
        parts = [part[:size] + exchange(part[size:], step) for part in parts]
    return jnp.concatenate(parts, axis=1) + returned


def solution(mesh):
    placed = (P("blk", None), P("blk", "split", None))
    return jax.shard_map(
        per_device, mesh=mesh, in_specs=placed, out_specs=P(("blk", "split"), None), check_vma=False
    )
```
